32 devices in a mesh: section: 4 (over y, core), fsdp: 2 (over x), seq: 4 (over z).
Axes of the slice: x: 2, y: 2, z: 4, core: 2. Of those that a mesh axis runs over, the one named last changes fastest.
Arguments:
- hidden: bfloat16 [4, 2048, 8192], P('section', ('fsdp', 'seq')), may hold values from -6 to 6
- queries: bfloat16 [4, 2048, 4096], P('section', ('fsdp', 'seq')), may hold values from -6 to 6
- kv_weight: bfloat16 [4, 8192, 1024], P('section', ('fsdp', 'seq')), may hold values from -0.0625 to 0.0625
- readout: float32 [4, 4096], P('section'), may hold values from -6 to 6
- segments: int32 [2, 1024], P('fsdp'), may hold values from 0 to 3, never falling along the last dimension, each value on 1 to 512 neighbouring positions
- block_mask: int32 [2, 8, 8], P('fsdp', 'seq'), may hold values 0 or 1
- response: int32 [2048], P(('fsdp', 'seq')), may hold values 0 or 1
Outputs:
- scores: float32 [4, 2048], P('section', ('fsdp', 'seq'))
- query_grad: bfloat16 [4, 2048, 4096], P('section', ('fsdp', 'seq'))
The draws below stay inside these ranges and needn't reach their ends.
All inputs are finite; a program needn't handle non-finite values. No bound on the sum of `block_mask` or of `response` on one device may be relied on, other than what follows from the above.
Results may differ from the reference program's by a relative error of at most 0.02.
Values may be sent and summed in bfloat16 or wider, within the bound.
A program may use at most 128 MiB of HBM per device.

```python
import math
import jax
import jax.numpy as jnp
import numpy as np
from jax import lax

D = 8192
QH = 32
KVH = 4
HD = 128
BLK = 128
KVW = 512
QW = 4096
SEQ_LEN = 1024
NBLK = 8
SEQS = 2
TOKENS = 2048
N_SECTION = 4


def set_ends(values, stream_key, low, top_value):
    place = [jax.random.randint(jax.random.fold_in(stream_key, axis), (), 0, length) for axis, length in enumerate(values.shape)]
    main_axis = values.shape.index(max(values.shape))
    neighbour = place[:main_axis] + [(place[main_axis] + 1) % values.shape[main_axis]] + place[main_axis + 1:]
    return values.at[tuple(place)].set(low).at[tuple(neighbour)].set(top_value)


def steps_of(stream_key, dims, pieces, smallest, high):
    def one(position, shards_of):
        heights = jax.random.uniform(jax.random.fold_in(jax.random.fold_in(stream_key, 6), position), (shards_of,), jnp.float32, smallest / len(pieces), high / len(pieces))
        return jnp.repeat(jnp.exp(heights), dims[position] // shards_of).reshape((-1,) + (1,) * (len(dims) - position - 1))

    gain = one(*pieces[0])
    for cut in pieces[1:]:
        gain = gain * one(*cut)
    return gain


def split_up(number_of, total, most, slope):
    portions = [(1 << 20) // math.isqrt(grade ** slope) + 1 for grade in range(2, number_of + 1)]
    spare, given = total - most - (number_of - 1), [1] * (number_of - 1)
    while spare > 0:
        free = [i for i in range(number_of - 1) if given[i] < most]
        mass, remaining = sum([portions[i] for i in free]), spare
        for i in free:
            addition = min(most - given[i], max(1, remaining * portions[i] // mass), spare)
            given[i] = given[i] + addition
            spare = spare - addition
    return np.array([most] + given)


def ragged_sizes(key, number_of, total, reach, skew):
    if number_of == 2:
        one = jax.random.randint(key, (), max(1, total - reach), min(reach, total - 1) + 1)
        return jnp.stack([one, total - one])
    sizes = jnp.asarray(split_up(number_of, total, reach, skew), jnp.int32)
    pairs = (number_of - 1) // 2
    source_of, sink = sizes[1:1 + 2 * pairs:2], sizes[2:2 + 2 * pairs:2]
    slack = jnp.minimum(source_of - 1, reach - sink)
    passed = jax.random.randint(jax.random.fold_in(key, 1), (pairs,), 0, 1 << 20) % (slack + 1)
    sizes = sizes.at[1:1 + 2 * pairs:2].set(source_of - passed).at[2:2 + 2 * pairs:2].set(sink + passed)
    return sizes[jax.random.permutation(jax.random.fold_in(key, 2), number_of)]


def gaussian(rng, dims, spread, reach, split=(), held_as=jnp.bfloat16):
    factor_of = steps_of(rng, dims, split, -0.22, 0.18) if split else 1.0
    values = jax.random.normal(rng, dims, jnp.float32) * spread * factor_of
    return jnp.minimum(jnp.maximum(values, -reach), reach).astype(held_as)


def setup_inputs(seed: int = 0) -> dict:
    key_of = jax.random.split(jax.random.key(seed), 8)
    return {
        "hidden": gaussian(key_of[0], (N_SECTION, TOKENS, D), 1.0, 6.0, ((0, 4), (1, 8))),
        "queries": gaussian(key_of[1], (N_SECTION, TOKENS, QW), 1.0, 6.0, ((0, 4), (1, 8))),
        "kv_weight": gaussian(key_of[2], (N_SECTION, D, 2 * KVW), D ** -0.5, 0.0625, ((0, 4), (1, 8))),
        "readout": gaussian(key_of[3], (N_SECTION, QW), 1.0, 6.0, ((0, 4),), jnp.float32),
        "segments": jax.vmap(lambda own: jnp.searchsorted(jnp.cumsum(ragged_sizes(own, 4, SEQ_LEN, SEQ_LEN // 2, 1)), jnp.arange(SEQ_LEN), side="right"))(jax.random.split(key_of[4], SEQS)).reshape((SEQS, SEQ_LEN)).astype(jnp.int32),
        "block_mask": set_ends((jax.random.randint(key_of[5], (SEQS, NBLK, NBLK), 0, 4) < 3).astype(jnp.int32), jax.random.fold_in(key_of[5], 1), 0, 1),
        "response": set_ends((jax.random.randint(key_of[6], (TOKENS,), 0, 3) < 2).astype(jnp.int32), jax.random.fold_in(key_of[6], 1), 0, 1),
    }


penalty_weight = 0.5

def reference(hidden, queries, kv_weight, readout, segments, block_mask, response):
    group_size = QH // KVH
    kv_width = KVH * HD
    score_scale = 1.0 / math.sqrt(HD)
    projected = lax.map(lambda pair: jnp.dot(pair[0], pair[1], preferred_element_type=jnp.float32).astype(jnp.bfloat16), (hidden, kv_weight))
    positions = jnp.arange(SEQ_LEN, dtype=jnp.int32)
    blocks = positions // BLK
    same_block = blocks[:, None] == blocks[None, :]
    causal = positions[None, :] <= positions[:, None]

    def forward(item_index):
        section = item_index // SEQS
        sequence = item_index % SEQS
        row_start = (sequence * SEQ_LEN).astype(jnp.int32)
        kv_rows = lax.dynamic_slice_in_dim(lax.dynamic_index_in_dim(projected, section, 0, False), row_start, SEQ_LEN, 0).astype(jnp.float32)
        key_rows = kv_rows[:, :kv_width].reshape(SEQ_LEN, KVH, HD)
        values = kv_rows[:, kv_width:].reshape(SEQ_LEN, KVH, HD)
        query_rows = lax.dynamic_slice_in_dim(lax.dynamic_index_in_dim(queries, section, 0, False), row_start, SEQ_LEN, 0).astype(jnp.float32).reshape(SEQ_LEN, KVH, group_size, HD)
        doc_ids = lax.dynamic_index_in_dim(segments, sequence, 0, False)
        block_table = jnp.repeat(jnp.repeat(lax.dynamic_index_in_dim(block_mask, sequence, 0, False), BLK, axis=0), BLK, axis=1)
        allowed = (doc_ids[:, None] == doc_ids[None, :]) & causal & ((block_table == 1) | same_block)
        logits = jnp.einsum('ikgd,jkd->kgij', query_rows, key_rows) * score_scale
        weights = jnp.where(allowed[None, None], jnp.exp(logits), 0.0)
        denominator = jnp.transpose(lax.optimization_barrier(jnp.sum(weights, axis=-1)), (2, 0, 1))
        rounded = weights.astype(jnp.bfloat16)
        summed = jnp.einsum('kgij,jkd->ikgd', rounded.astype(jnp.float32), values)
        attended = summed / denominator[..., None]
        read_gains = lax.dynamic_index_in_dim(readout, section, 0, False).astype(jnp.float32).reshape(KVH, group_size, HD)
        head_scores = lax.optimization_barrier(jnp.sum(attended * read_gains, axis=-1))
        return (weights, rounded, denominator, head_scores, key_rows, values, read_gains)

    def score_of(item_index):
        head_scores = forward(item_index)[3]
        return lax.optimization_barrier(jnp.sum(head_scores, axis=(1, 2)))
    items = jnp.arange(N_SECTION * SEQS, dtype=jnp.int32)
    scores = lax.map(score_of, items).reshape(N_SECTION, TOKENS)
    live_rows = response.astype(jnp.float32)
    actor_grad = live_rows * (penalty_weight * (scores[0] - scores[1]) - (scores[2] - scores[3]))
    critic_grad = live_rows * (scores[3] - scores[2])
    no_grad = jnp.zeros_like(live_rows)
    loss_grad = jnp.stack([actor_grad, no_grad, no_grad, critic_grad])

    def grad_of(item_index):
        weights, rounded, denominator, head_scores, key_rows, values, read_gains = forward(item_index)
        section = item_index // SEQS
        sequence = item_index % SEQS
        grad_rows = lax.dynamic_slice_in_dim(lax.dynamic_index_in_dim(loss_grad, section, 0, False), (sequence * SEQ_LEN).astype(jnp.int32), SEQ_LEN, 0)
        value_gain = jnp.einsum('jkd,kgd->jkg', values, read_gains)
        scaled = (weights * jnp.transpose(value_gain, (1, 2, 0))[:, :, None, :]).astype(jnp.bfloat16)
        first_sum = jnp.einsum('kgij,jkd->ikgd', scaled.astype(jnp.float32), key_rows)
        second_sum = jnp.einsum('kgij,jkd->ikgd', rounded.astype(jnp.float32), key_rows)
        factor = score_scale * grad_rows[:, None, None] / denominator
        result = factor[..., None] * (first_sum - head_scores[..., None] * second_sum)
        return result.reshape(SEQ_LEN, QH * HD).astype(jnp.bfloat16)
    query_grad = lax.map(grad_of, items).reshape(N_SECTION, TOKENS, QH * HD)
    return (scores, query_grad)
```

```python
import functools
import math

import jax
import jax.numpy as jnp
from jax import lax
from jax.experimental import pallas as pl
from jax.experimental.pallas import tpu as pltpu
from jax.sharding import PartitionSpec as P

QH = 32
KVH = 4
HD = 128
BLK = 128
CHUNKS = 4
HIDE = -1e30

penalty_weight = 0.5
MESH = pl.DeviceIdType.MESH


def project_kernel(
    f, n, wb, hidden, weight, out,
    hid, wts, part, rs, own, kvw,
    hid_send, hid_recv, w_send, w_recv, rs_send, rs_recv, ag_send, ag_recv, local_sem,
):
    rows = hidden.shape[0]
    slab = weight.shape[0]
    cols = weight.shape[1] // CHUNKS
    hs = n // 2
    group = f * hs
    fx = lax.axis_index("fsdp")
    sq = lax.axis_index("seq")
    half = sq // hs
    zz = sq % hs
    gi = fx * hs + zz
    mirror = (1 - half) * hs + zz

    def member(d):
        g = (gi + d) % group
        return g // hs, g % hs

    def hid_slice(mf, mz, side):
        place = jnp.where(side == 0, half, 1 - half)
        start = (mf * n + place * hs + mz) * slab
        return hidden.at[:, pl.ds(pl.multiple_of(start, 128), slab)]

    def hid_copy(d, side):
        mf, mz = member(d)
        return pltpu.make_async_remote_copy(
            src_ref=hid_slice(mf, mz, side),
            dst_ref=hid.at[side, group - d],
            send_sem=hid_send.at[side, d],
            recv_sem=hid_recv.at[side, group - d],
            device_id={"fsdp": mf, "seq": half * hs + mz},
            device_id_type=MESH,
        )

    def hid_arrival(d, side):
        mf, mz = member(d)
        return pltpu.make_async_remote_copy(
            src_ref=hid_slice(mf, mz, side),
            dst_ref=hid.at[side, d],
            send_sem=hid_send.at[side, d],
            recv_sem=hid_recv.at[side, d],
            device_id={"fsdp": mf, "seq": half * hs + mz},
            device_id_type=MESH,
        )

    def w_copy(c):
        return pltpu.make_async_remote_copy(
            src_ref=weight.at[:, c * cols:(c + 1) * cols],
            dst_ref=wts.at[1, c],
            send_sem=w_send.at[c],
            recv_sem=w_recv.at[c],
            device_id={"seq": mirror},
            device_id_type=MESH,
        )

    def rs_copy(c, d):
        mf, mz = member(d)
        return pltpu.make_async_remote_copy(
            src_ref=part.at[c, d],
            dst_ref=rs.at[c, group - d],
            send_sem=rs_send.at[c, d],
            recv_sem=rs_recv.at[c, group - d],
            device_id={"fsdp": mf, "seq": half * hs + mz},
            device_id_type=MESH,
        )

    def rs_arrival(c, d):
        mf, mz = member(d)
        return pltpu.make_async_remote_copy(
            src_ref=part.at[c, d],
            dst_ref=rs.at[c, d],
            send_sem=rs_send.at[c, d],
            recv_sem=rs_recv.at[c, d],
            device_id={"fsdp": mf, "seq": half * hs + mz},
            device_id_type=MESH,
        )

    def ag_copy(c, j):
        return pltpu.make_async_remote_copy(
            src_ref=kvw.at[wb, c],
            dst_ref=kvw.at[wb - j, c],
            send_sem=ag_send.at[c, j - 1],
            recv_sem=ag_recv.at[c, j - 1],
            device_id={"seq": (sq + j) % n},
            device_id_type=MESH,
        )

    own_w = [
        pltpu.make_async_copy(
            weight.at[:, c * cols:(c + 1) * cols], wts.at[0, c], local_sem.at[2 + c]
        )
        for c in range(CHUNKS)
    ]
    own_h = [
        pltpu.make_async_copy(hid_slice(fx, zz, side), hid.at[side, 0], local_sem.at[side])
        for side in range(2)
    ]

    barrier = pltpu.get_barrier_semaphore()
    everyone = f * n
    me = fx * n + sq

    def greet(d, carry):
        other = (me + d) % everyone
        pl.semaphore_signal(
            barrier, inc=1, device_id={"fsdp": other // n, "seq": other % n}, device_id_type=MESH
        )
        return carry

    lax.fori_loop(1, everyone, greet, 0)
    pl.semaphore_wait(barrier, everyone - 1)

    def send_hidden(d, carry):
        hid_copy(d, 0).start()
        hid_copy(d, 1).start()
        return carry

    lax.fori_loop(1, group, send_hidden, 0)
    for c in range(CHUNKS):
        w_copy(c).start()
    for copy in own_h + own_w:
        copy.start()

    for j in range(1, wb + 1):
        @pl.when(sq < j)
        def _():
            kvw[wb - j] = jnp.zeros_like(kvw[wb - j])

    for copy in own_h + own_w:
        copy.wait()

    def take_hidden(d, carry):
        hid_arrival(d, 0).wait_recv()
        hid_arrival(d, 1).wait_recv()
        return carry

    lax.fori_loop(1, group, take_hidden, 0)

    def product(c, d):
        return jnp.dot(hid[0, d], wts[0, c], preferred_element_type=jnp.float32) + jnp.dot(
            hid[1, d], wts[1, c], preferred_element_type=jnp.float32
        )

    def finish(c):
        def add(d, carry):
            rs_arrival(c, d).wait_recv()
            own[c] += rs[c, d].astype(jnp.float32)
            return carry

        lax.fori_loop(1, group, add, 0)
        kvw[wb, c] = own[c].astype(jnp.bfloat16)
        for j in range(1, wb + 1):
            @pl.when(sq + j < n)
            def _():
                ag_copy(c, j).start()

    for c in range(CHUNKS):
        w_copy(c).wait_recv()

        def spread(d, carry):
            part[c, d] = product(c, d).astype(jnp.bfloat16)
            rs_copy(c, d).start()
            return carry

        lax.fori_loop(1, group, spread, 0)
        own[c] = product(c, 0)
        if c > 0:
            finish(c - 1)
    finish(CHUNKS - 1)

    def sent(d, carry):
        hid_copy(d, 0).wait_send()
        hid_copy(d, 1).wait_send()
        for c in range(CHUNKS):
            rs_copy(c, d).wait_send()
        return carry

    lax.fori_loop(1, group, sent, 0)
    for c in range(CHUNKS):
        w_copy(c).wait_send()
        for j in range(1, wb + 1):
            @pl.when(sq >= j)
            def _():
                ag_copy(c, j).wait_recv()

            @pl.when(sq + j < n)
            def _():
                ag_copy(c, j).wait_send()
    for s in range(wb + 1):
        for c in range(CHUNKS):
            out[s * rows:(s + 1) * rows, c * cols:(c + 1) * cols] = kvw[s, c]


def project(hidden, weight, f, n, wb):
    rows = hidden.shape[0]
    slab, width = weight.shape
    group = f * (n // 2)
    cols = width // CHUNKS
    dma = pltpu.SemaphoreType.DMA
    return pl.pallas_call(
        functools.partial(project_kernel, f, n, wb),
        out_shape=jax.ShapeDtypeStruct(((wb + 1) * rows, width), jnp.bfloat16),
        in_specs=[pl.BlockSpec(memory_space=pl.ANY)] * 2,
        out_specs=pl.BlockSpec(memory_space=pltpu.VMEM),
        scratch_shapes=[
            pltpu.VMEM((2, group, rows, slab), jnp.bfloat16),
            pltpu.VMEM((2, CHUNKS, slab, cols), jnp.bfloat16),
            pltpu.VMEM((CHUNKS, group, rows, cols), jnp.bfloat16),
            pltpu.VMEM((CHUNKS, group, rows, cols), jnp.bfloat16),
            pltpu.VMEM((CHUNKS, rows, cols), jnp.float32),
            pltpu.VMEM((wb + 1, CHUNKS, rows, cols), jnp.bfloat16),
            dma((2, group)), dma((2, group)),
            dma((CHUNKS,)), dma((CHUNKS,)),
            dma((CHUNKS, group)), dma((CHUNKS, group)),
            dma((CHUNKS, wb)), dma((CHUNKS, wb)),
            dma((2 + CHUNKS,)),
        ],
        compiler_params=pltpu.CompilerParams(
            collective_id=0, has_side_effects=True, vmem_limit_bytes=56 * 1024 * 1024
        ),
        cost_estimate=pl.CostEstimate(
            flops=2 * group * rows * 2 * slab * width,
            bytes_accessed=2 * rows * hidden.shape[1] + 4 * slab * width,
            transcendentals=0,
        ),
    )(hidden, weight)


def attend_kernel(blocks, first, q, keys, values, gains, q_doc, k_doc, grad, scores, bias):
    rows, window = bias.shape
    heads = gains.shape[0]
    scale = 1.0 / math.sqrt(HD)
    step = pl.program_id(0)

    @pl.when(step == 0)
    def _():
        ahead = window - rows
        for a in range(rows // BLK):
            for b in range(window // BLK):
                own = b == a + ahead // BLK
                if b > a + ahead // BLK:
                    seen = jnp.zeros((BLK, BLK), jnp.bool_)
                else:
                    seen = q_doc[a * BLK:(a + 1) * BLK, :] == k_doc[:, b * BLK:(b + 1) * BLK]
                    if own:
                        i = lax.broadcasted_iota(jnp.int32, (BLK, BLK), 0)
                        j = lax.broadcasted_iota(jnp.int32, (BLK, BLK), 1)
                        seen = seen & (j <= i)
                place = first[0] + b
                bias[a * BLK:(a + 1) * BLK, b * BLK:(b + 1) * BLK] = jnp.where(seen, 0.0, HIDE)
                if b < a + ahead // BLK:
                    shut = (place < 0) | (blocks[a, jnp.maximum(place, 0)] != 1)

                    @pl.when(shut)
                    def _():
                        bias[a * BLK:(a + 1) * BLK, b * BLK:(b + 1) * BLK] = jnp.full(
                            (BLK, BLK), HIDE, jnp.float32
                        )
        scores[...] = jnp.zeros_like(scores)

    k = keys[...]
    gain = lax.dot_general(
        gains[...], values[...].astype(jnp.float32), (((1,), (1,)), ((), ())),
        precision=lax.Precision.HIGHEST, preferred_element_type=jnp.float32,
    )
    total = jnp.zeros((rows, 1), jnp.float32)
    for h in range(heads):
        logits = lax.dot_general(
            q[:, h * HD:(h + 1) * HD], k, (((1,), (1,)), ((), ())),
            preferred_element_type=jnp.float32,
        )
        p = jnp.exp2(logits * (scale * math.log2(math.e)) + bias[...])
        u = gain[h:h + 1, :]
        den = jnp.sum(p, axis=1, keepdims=True)
        inverse = 1.0 / den
        rho = jnp.sum(p * u, axis=1, keepdims=True) * inverse
        pulled = (p * (u - rho)).astype(jnp.bfloat16)
        moved = jnp.dot(pulled, k, preferred_element_type=jnp.float32)
        grad[:, h * HD:(h + 1) * HD] = (moved * (scale * inverse)).astype(grad.dtype)
        total = total + rho
    scores[...] += total


def attend(q, kv, gains, q_doc, k_doc, blocks, first):
    rows, width = q.shape
    window = kv.shape[0]
    group_size = QH // KVH
    smem = pl.BlockSpec(memory_space=pltpu.SMEM)
    return pl.pallas_call(
        attend_kernel,
        grid=(KVH,),
        out_shape=(
            jax.ShapeDtypeStruct((rows, width), jnp.bfloat16),
            jax.ShapeDtypeStruct((rows, 1), jnp.float32),
        ),
        in_specs=[
            smem,
            smem,
            pl.BlockSpec((rows, group_size * HD), lambda s: (0, s)),
            pl.BlockSpec((window, HD), lambda s: (0, s)),
            pl.BlockSpec((window, HD), lambda s: (0, KVH + s)),
            pl.BlockSpec((group_size, HD), lambda s: (s, 0)),
            pl.BlockSpec((rows, 1), lambda s: (0, 0)),
            pl.BlockSpec((1, window), lambda s: (0, 0)),
        ],
        out_specs=(
            pl.BlockSpec((rows, group_size * HD), lambda s: (0, s)),
            pl.BlockSpec((rows, 1), lambda s: (0, 0)),
        ),
        scratch_shapes=[pltpu.VMEM((rows, window), jnp.float32)],
        compiler_params=pltpu.CompilerParams(vmem_limit_bytes=48 * 1024 * 1024),
        cost_estimate=pl.CostEstimate(
            flops=4 * rows * width * window,
            bytes_accessed=4 * rows * width + 2 * window * 2 * KVH * HD,
            transcendentals=rows * window * QH,
        ),
    )(blocks, first, q, kv, kv, gains, q_doc, k_doc)


def on_device(hidden, queries, kv_weight, readout, segments, block_mask, response):
    rows = hidden.shape[1]
    f = lax.axis_size("fsdp")
    n = lax.axis_size("seq")
    seq_len = segments.shape[1]
    wb = -(-(seq_len // 2 - 1) // rows)
    sq = lax.axis_index("seq")
    kv = project(hidden[0], kv_weight[0], f, n, wb)
    docs = jnp.concatenate([jnp.full((1, wb * rows), -1, jnp.int32), segments], axis=1)
    k_doc = lax.dynamic_slice_in_dim(docs, sq * rows, (wb + 1) * rows, 1)
    q_doc = k_doc[:, wb * rows:].reshape(rows, 1)
    first = ((sq - wb) * (rows // BLK)).astype(jnp.int32).reshape(1)
    grad, token_scores = attend(
        queries[0], kv, readout[0].reshape(QH, HD), q_doc, k_doc, block_mask[0], first
    )
    token_scores = token_scores.reshape(1, rows)
    joined = lax.all_gather(token_scores, "section", axis=0, tiled=True)
    section_index = lax.axis_index("section")
    actor_part = (section_index == 0).astype(jnp.float32)
    critic_part = (section_index == 3).astype(jnp.float32)
    live_rows = response.astype(jnp.float32)
    actor_term = penalty_weight * (joined[0] - joined[1]) - (joined[2] - joined[3])
    critic_term = joined[3] - joined[2]
    loss_grad = live_rows * (actor_part * actor_term + critic_part * critic_term)
    query_grad = (loss_grad[:, None] * grad.astype(jnp.float32)).astype(jnp.bfloat16)
    return (token_scores, query_grad[None])


def solution(mesh):
    placed = (
        P("section", ("fsdp", "seq"), None),
        P("section", ("fsdp", "seq"), None),
        P("section", ("fsdp", "seq"), None),
        P("section", None),
        P("fsdp", None),
        P("fsdp", "seq", None),
        P(("fsdp", "seq")),
    )
    return jax.shard_map(
        on_device,
        mesh=mesh,
        in_specs=placed,
        out_specs=(P("section", ("fsdp", "seq")), P("section", ("fsdp", "seq"), None)),
        check_vma=False,
    )
```

```python
import functools
import math

import jax
import jax.numpy as jnp
from jax import lax
from jax.experimental import pallas as pl
from jax.experimental.pallas import tpu as pltpu
from jax.sharding import PartitionSpec as P

QH = 32
KVH = 4
HD = 128
BLK = 128
CHUNKS = KVH
HIDE = -1e30

penalty_weight = 0.5
MESH = pl.DeviceIdType.MESH


def step_kernel(
    f, n, wb, sections, hidden, weight, queries, gains, q_doc, k_doc, opened, live,
    grad, scores, factor,
    hid, wts, part, rs, own, kvw, q, moved, bias, gain, joined,
    hid_send, hid_recv, w_send, w_recv, rs_send, rs_recv, ag_send, ag_recv,
    join_send, join_recv, local_sem, grad_sem,
):
    rows = hidden.shape[0]
    slab = weight.shape[0]
    cols = weight.shape[1] // CHUNKS
    hs = n // 2
    group = f * hs
    fx = lax.axis_index("fsdp")
    sq = lax.axis_index("seq")
    half = sq // hs
    zz = sq % hs
    gi = fx * hs + zz
    mirror = (1 - half) * hs + zz
    sec = lax.axis_index("section")

    def member(d):
        g = (gi + d) % group
        return g // hs, g % hs

    def hid_slice(mf, mz, side):
        place = jnp.where(side == 0, half, 1 - half)
        start = (mf * n + place * hs + mz) * slab
        return hidden.at[:, pl.ds(pl.multiple_of(start, 128), slab)]

    def hid_copy(d, side):
        mf, mz = member(d)
        return pltpu.make_async_remote_copy(
            src_ref=hid_slice(mf, mz, side),
            dst_ref=hid.at[side, group - d],
            send_sem=hid_send.at[side, d],
            recv_sem=hid_recv.at[side, group - d],
            device_id={"fsdp": mf, "seq": half * hs + mz},
            device_id_type=MESH,
        )

    def hid_arrival(d, side):
        mf, mz = member(d)
        return pltpu.make_async_remote_copy(
            src_ref=hid_slice(mf, mz, side),
            dst_ref=hid.at[side, d],
            send_sem=hid_send.at[side, d],
            recv_sem=hid_recv.at[side, d],
            device_id={"fsdp": mf, "seq": half * hs + mz},
            device_id_type=MESH,
        )

    def w_slice(c, t):
        start = (t * KVH + c) * HD
        return weight.at[:, start:start + HD]

    def w_copy(c, t):
        return pltpu.make_async_remote_copy(
            src_ref=w_slice(c, t),
            dst_ref=wts.at[1, c, :, t * HD:(t + 1) * HD],
            send_sem=w_send.at[c, t],
            recv_sem=w_recv.at[c, t],
            device_id={"seq": mirror},
            device_id_type=MESH,
        )

    def rs_copy(c, d):
        mf, mz = member(d)
        return pltpu.make_async_remote_copy(
            src_ref=part.at[c, d],
            dst_ref=rs.at[c, group - d],
            send_sem=rs_send.at[c, d],
            recv_sem=rs_recv.at[c, group - d],
            device_id={"fsdp": mf, "seq": half * hs + mz},
            device_id_type=MESH,
        )

    def rs_arrival(c, d):
        mf, mz = member(d)
        return pltpu.make_async_remote_copy(
            src_ref=part.at[c, d],
            dst_ref=rs.at[c, d],
            send_sem=rs_send.at[c, d],
            recv_sem=rs_recv.at[c, d],
            device_id={"fsdp": mf, "seq": half * hs + mz},
            device_id_type=MESH,
        )

    def ag_copy(c, j):
        return pltpu.make_async_remote_copy(
            src_ref=kvw.at[wb, c],
            dst_ref=kvw.at[wb - j, c],
            send_sem=ag_send.at[c, j - 1],
            recv_sem=ag_recv.at[c, j - 1],
            device_id={"seq": (sq + j) % n},
            device_id_type=MESH,
        )

    own_w = [
        pltpu.make_async_copy(
            w_slice(c, t), wts.at[0, c, :, t * HD:(t + 1) * HD], local_sem.at[2 + 2 * c + t]
        )
        for c in range(CHUNKS)
        for t in range(2)
    ]
    own_q = pltpu.make_async_copy(queries, q, local_sem.at[2 + 2 * CHUNKS])

    def join_copy(d):
        return pltpu.make_async_remote_copy(
            src_ref=joined.at[sec],
            dst_ref=joined.at[sec],
            send_sem=join_send.at[d],
            recv_sem=join_recv.at[sections - d],
            device_id={"section": (sec + d) % sections},
            device_id_type=MESH,
        )

    def join_arrival(d):
        return pltpu.make_async_remote_copy(
            src_ref=joined.at[sec],
            dst_ref=joined.at[(sec + d) % sections],
            send_sem=join_send.at[d],
            recv_sem=join_recv.at[d],
            device_id={"section": (sec + d) % sections},
            device_id_type=MESH,
        )

    def grad_copy(c):
        wide = gains.shape[0] // KVH * HD
        return pltpu.make_async_copy(
            moved.at[c], grad.at[:, c * wide:(c + 1) * wide], grad_sem.at[c]
        )

    own_h = [
        pltpu.make_async_copy(hid_slice(fx, zz, side), hid.at[side, 0], local_sem.at[side])
        for side in range(2)
    ]

    barrier = pltpu.get_barrier_semaphore()
    everyone = f * n
    me = fx * n + sq

    def greet(d, carry):
        other = (me + d) % everyone
        pl.semaphore_signal(
            barrier, inc=1, device_id={"fsdp": other // n, "seq": other % n}, device_id_type=MESH
        )
        return carry

    lax.fori_loop(1, everyone, greet, 0)
    for d in range(1, sections):
        pl.semaphore_signal(
            barrier, inc=1, device_id={"section": (sec + d) % sections}, device_id_type=MESH
        )
    pl.semaphore_wait(barrier, everyone - 1 + sections - 1)

    def send_hidden(d, carry):
        hid_copy(d, 0).start()
        hid_copy(d, 1).start()
        return carry

    lax.fori_loop(1, group, send_hidden, 0)
    for c in range(CHUNKS):
        w_copy(c, 0).start()
        w_copy(c, 1).start()
    for copy in own_h + own_w + [own_q]:
        copy.start()

    window = (wb + 1) * rows
    i = lax.broadcasted_iota(jnp.int32, (BLK, window), 0)
    j = lax.broadcasted_iota(jnp.int32, (BLK, window), 1) - wb * rows
    for a in range(rows // BLK):
        seen = q_doc[a * BLK:(a + 1) * BLK, :] == k_doc[...]
        seen = seen & (j <= i + a * BLK)
        seen = seen & ((opened[a:a + 1, :] == 1) | (j >= a * BLK))
        bias[a * BLK:(a + 1) * BLK, :] = jnp.where(seen, 0.0, HIDE)

    for j in range(1, wb + 1):
        @pl.when(sq < j)
        def _():
            kvw[wb - j] = jnp.zeros_like(kvw[wb - j])

    for copy in own_h + own_w + [own_q]:
        copy.wait()

    def take_hidden(d, carry):
        hid_arrival(d, 0).wait_recv()
        hid_arrival(d, 1).wait_recv()
        return carry

    lax.fori_loop(1, group, take_hidden, 0)

    def product(c, d):
        return jnp.dot(hid[0, d], wts[0, c], preferred_element_type=jnp.float32) + jnp.dot(
            hid[1, d], wts[1, c], preferred_element_type=jnp.float32
        )

    def finish(c):
        def add(d, carry):
            rs_arrival(c, d).wait_recv()
            own[c] += rs[c, d].astype(jnp.float32)
            return carry

        lax.fori_loop(1, group, add, 0)
        kvw[wb, c] = own[c].astype(jnp.bfloat16)
        for j in range(1, wb + 1):
            @pl.when(sq + j < n)
            def _():
                ag_copy(c, j).start()

    scale = 1.0 / math.sqrt(HD)
    heads = gains.shape[0] // KVH

    def attend(c, total):
        for j in range(1, wb + 1):
            @pl.when(sq >= j)
            def _():
                ag_copy(c, j).wait_recv()

        k = kvw[:, c, :, :HD].reshape(window, HD)
        v = kvw[:, c, :, HD:].reshape(window, HD)
        gain[...] = lax.dot_general(
            gains[c * heads:(c + 1) * heads, :], v.astype(jnp.float32), (((1,), (1,)), ((), ())),
            precision=lax.Precision.HIGHEST, preferred_element_type=jnp.float32,
        )

        def head(h, total):
            start = pl.multiple_of((c * heads + h) * HD, HD)
            logits = lax.dot_general(
                q[:, pl.ds(start, HD)], k, (((1,), (1,)), ((), ())),
                preferred_element_type=jnp.float32,
            )
            p = jnp.exp2(logits * (scale * math.log2(math.e)) + bias[...])
            u = gain[pl.ds(h, 1), :]
            inverse = 1.0 / jnp.sum(p, axis=1, keepdims=True)
            rho = jnp.sum(p * u, axis=1, keepdims=True) * inverse
            pulled = (p * (u - rho)).astype(jnp.bfloat16)
            pull = jnp.dot(pulled, k, preferred_element_type=jnp.float32) * (scale * inverse)
            moved[c, :, pl.ds(pl.multiple_of(h * HD, HD), HD)] = pull.astype(jnp.bfloat16)
            return total + rho

        def pair(t, total):
            return head(2 * t + 1, head(2 * t, total))

        total = lax.fori_loop(0, heads // 2, pair, total)
        grad_copy(c).start()
        return total

    total = jnp.zeros((rows, 1), jnp.float32)
    for c in range(CHUNKS):
        w_copy(c, 0).wait_recv()
        w_copy(c, 1).wait_recv()

        def spread(d, carry):
            part[c, d] = product(c, d).astype(jnp.bfloat16)
            rs_copy(c, d).start()
            return carry

        lax.fori_loop(1, group, spread, 0)
        own[c] = product(c, 0)
        if c > 0:
            finish(c - 1)
        if c > 1:
            total = attend(c - 2, total)
    finish(CHUNKS - 1)
    total = attend(CHUNKS - 2, total)
    total = attend(CHUNKS - 1, total)

    row = jnp.transpose(jnp.broadcast_to(total, (rows, HD)))[:8, :]
    joined[sec] = row
    scores[...] = row[:1, :]
    for d in range(1, sections):
        join_copy(d).start()

    def sent(d, carry):
        hid_copy(d, 0).wait_send()
        hid_copy(d, 1).wait_send()
        for c in range(CHUNKS):
            rs_copy(c, d).wait_send()
        return carry

    lax.fori_loop(1, group, sent, 0)
    for c in range(CHUNKS):
        w_copy(c, 0).wait_send()
        w_copy(c, 1).wait_send()
        grad_copy(c).wait()
        for j in range(1, wb + 1):
            @pl.when(sq + j < n)
            def _():
                ag_copy(c, j).wait_send()
    for d in range(1, sections):
        join_copy(d).wait_send()
        join_arrival(d).wait_recv()
    by_model = [joined[m, :1, :] for m in range(4)]
    actor_part = (sec == 0).astype(jnp.float32)
    critic_part = (sec == 3).astype(jnp.float32)
    actor_term = penalty_weight * (by_model[0] - by_model[1]) - (by_model[2] - by_model[3])
    critic_term = by_model[3] - by_model[2]
    factor[...] = live[...].astype(jnp.float32) * (
        actor_part * actor_term + critic_part * critic_term
    )


def run_step(hidden, weight, queries, gains, q_doc, k_doc, opened, live, f, n, wb, sections):
    rows = hidden.shape[0]
    slab, width = weight.shape
    group = f * (n // 2)
    cols = width // CHUNKS
    window = (wb + 1) * rows
    wide = queries.shape[1] // KVH
    dma = pltpu.SemaphoreType.DMA
    hbm = pl.BlockSpec(memory_space=pl.ANY)
    vmem = pl.BlockSpec(memory_space=pltpu.VMEM)
    return pl.pallas_call(
        functools.partial(step_kernel, f, n, wb, sections),
        out_shape=(
            jax.ShapeDtypeStruct(queries.shape, jnp.bfloat16),
            jax.ShapeDtypeStruct((1, rows), jnp.float32),
            jax.ShapeDtypeStruct((1, rows), jnp.float32),
        ),
        in_specs=[hbm] * 3 + [vmem] * 5,
        out_specs=(hbm, vmem, vmem),
        scratch_shapes=[
            pltpu.VMEM((2, group, rows, slab), jnp.bfloat16),
            pltpu.VMEM((2, CHUNKS, slab, cols), jnp.bfloat16),
            pltpu.VMEM((CHUNKS, group, rows, cols), jnp.bfloat16),
            pltpu.VMEM((CHUNKS, group, rows, cols), jnp.bfloat16),
            pltpu.VMEM((CHUNKS, rows, cols), jnp.float32),
            pltpu.VMEM((wb + 1, CHUNKS, rows, cols), jnp.bfloat16),
            pltpu.VMEM(queries.shape, jnp.bfloat16),
            pltpu.VMEM((KVH, rows, wide), jnp.bfloat16),
            pltpu.VMEM((rows, window), jnp.float32),
            pltpu.VMEM((QH // KVH, window), jnp.float32),
            pltpu.VMEM((sections, 8, rows), jnp.float32),
            dma((2, group)), dma((2, group)),
            dma((CHUNKS, 2)), dma((CHUNKS, 2)),
            dma((CHUNKS, group)), dma((CHUNKS, group)),
            dma((CHUNKS, wb)), dma((CHUNKS, wb)),
            dma((sections,)), dma((sections,)),
            dma((3 + 2 * CHUNKS,)), dma((KVH,)),
        ],
        compiler_params=pltpu.CompilerParams(
            collective_id=0, has_side_effects=True, vmem_limit_bytes=58 * 1024 * 1024
        ),
        cost_estimate=pl.CostEstimate(
            flops=4 * group * rows * slab * width + 4 * rows * queries.shape[1] * window,
            bytes_accessed=2 * hidden.size + 4 * weight.size + 4 * queries.size,
            transcendentals=rows * window * QH,
        ),
    )(hidden, weight, queries, gains, q_doc, k_doc, opened, live)


def on_device(hidden, queries, kv_weight, readout, segments, block_mask, response):
    rows = hidden.shape[1]
    f = lax.axis_size("fsdp")
    n = lax.axis_size("seq")
    sections = lax.axis_size("section")
    seq_len = segments.shape[1]
    wb = -(-(seq_len // 2 - 1) // rows)
    sq = lax.axis_index("seq")
    docs = jnp.concatenate([jnp.full((1, wb * rows), -1, jnp.int32), segments], axis=1)
    k_doc = lax.dynamic_slice_in_dim(docs, sq * rows, (wb + 1) * rows, 1)
    q_doc = k_doc[:, wb * rows:].reshape(rows, 1)
    table = jnp.repeat(jnp.pad(block_mask[0], ((0, 0), (wb * rows // BLK, 0))), BLK, axis=1)
    opened = lax.dynamic_slice_in_dim(table, sq * rows, (wb + 1) * rows, 1)
    grad, token_scores, factor = run_step(
        hidden[0], kv_weight[0], queries[0], readout[0].reshape(QH, HD),
        q_doc, k_doc, opened, response.reshape(1, rows), f, n, wb, sections,
    )
    query_grad = (factor.reshape(rows, 1) * grad.astype(jnp.float32)).astype(jnp.bfloat16)
    return (token_scores, query_grad[None])


def solution(mesh):
    placed = (
        P("section", ("fsdp", "seq"), None),
        P("section", ("fsdp", "seq"), None),
        P("section", ("fsdp", "seq"), None),
        P("section", None),
        P("fsdp", None),
        P("fsdp", "seq", None),
        P(("fsdp", "seq")),
    )
    return jax.shard_map(
        on_device,
        mesh=mesh,
        in_specs=placed,
        out_specs=(P("section", ("fsdp", "seq")), P("section", ("fsdp", "seq"), None)),
        check_vma=False,
    )
```

```python
import functools
import math

import jax
import jax.numpy as jnp
from jax import lax
from jax.experimental import pallas as pl
from jax.experimental.pallas import tpu as pltpu
from jax.sharding import PartitionSpec as P

QH = 32
KVH = 4
HD = 128
BLK = 128
CHUNKS = KVH
HIDE = -1e30

penalty_weight = 0.5
MESH = pl.DeviceIdType.MESH


def step_kernel(
    f, n, wb, sections, hidden, weight, queries, gains, q_doc, k_doc, opened, live,
    grad, scores, factor,
    hid, wts, part, rs, part2, rs2, own, kvw, q, moved, bias, gain, joined,
    hid_send, hid_recv, w_send, w_recv, rs_send, rs_recv, al_send, al_recv, ag_send, ag_recv,
    join_send, join_recv, local_sem, grad_sem,
):
    rows = hidden.shape[0]
    slab = weight.shape[0]
    cols = weight.shape[1] // CHUNKS
    hs = n // 2
    group = f * hs
    fx = lax.axis_index("fsdp")
    sq = lax.axis_index("seq")
    half = sq // hs
    zz = sq % hs
    gi = fx * hs + zz
    mirror = (1 - half) * hs + zz
    sec = lax.axis_index("section")

    def member(d):
        g = (gi + d) % group
        return g // hs, g % hs

    def hid_slice(mf, mz, side):
        place = jnp.where(side == 0, half, 1 - half)
        start = (mf * n + place * hs + mz) * slab
        return hidden.at[:, pl.ds(pl.multiple_of(start, 128), slab)]

    def hid_copy(d, side):
        mf, mz = member(d)
        return pltpu.make_async_remote_copy(
            src_ref=hid_slice(mf, mz, side),
            dst_ref=hid.at[side, group - d],
            send_sem=hid_send.at[side, d],
            recv_sem=hid_recv.at[side, group - d],
            device_id={"fsdp": mf, "seq": half * hs + mz},
            device_id_type=MESH,
        )

    def hid_arrival(d, side):
        mf, mz = member(d)
        return pltpu.make_async_remote_copy(
            src_ref=hid_slice(mf, mz, side),
            dst_ref=hid.at[side, d],
            send_sem=hid_send.at[side, d],
            recv_sem=hid_recv.at[side, d],
            device_id={"fsdp": mf, "seq": half * hs + mz},
            device_id_type=MESH,
        )

    def w_slice(c, t):
        start = (t * KVH + c) * HD
        return weight.at[:, start:start + HD]

    def w_copy(c, t):
        return pltpu.make_async_remote_copy(
            src_ref=w_slice(c, t),
            dst_ref=wts.at[1, c, :, t * HD:(t + 1) * HD],
            send_sem=w_send.at[c, t],
            recv_sem=w_recv.at[c, t],
            device_id={"seq": mirror},
            device_id_type=MESH,
        )

    def rs_move(c, e, slot):
        df, dz = e // hs, e % hs
        return pltpu.make_async_remote_copy(
            src_ref=part.at[c, e - hs],
            dst_ref=rs.at[c, slot - hs],
            send_sem=rs_send.at[c, e - hs],
            recv_sem=rs_recv.at[c, slot - hs],
            device_id={"fsdp": (fx + df) % f},
            device_id_type=MESH,
        )

    def rs_copy(c, e):
        return rs_move(c, e, (f - e // hs) * hs + e % hs)

    def rs_arrival(c, e):
        return rs_move(c, e, e)

    def along_move(c, dz, slot):
        return pltpu.make_async_remote_copy(
            src_ref=part2.at[c, dz],
            dst_ref=rs2.at[c, slot],
            send_sem=al_send.at[c, dz],
            recv_sem=al_recv.at[c, slot],
            device_id={"seq": half * hs + (zz + dz) % hs},
            device_id_type=MESH,
        )

    def ag_copy(c, j):
        return pltpu.make_async_remote_copy(
            src_ref=kvw.at[wb, c],
            dst_ref=kvw.at[wb - j, c],
            send_sem=ag_send.at[c, j - 1],
            recv_sem=ag_recv.at[c, j - 1],
            device_id={"seq": (sq + j) % n},
            device_id_type=MESH,
        )

    own_w = [
        pltpu.make_async_copy(
            w_slice(c, t), wts.at[0, c, :, t * HD:(t + 1) * HD], local_sem.at[2 + 2 * c + t]
        )
        for c in range(CHUNKS)
        for t in range(2)
    ]
    own_q = pltpu.make_async_copy(queries, q, local_sem.at[2 + 2 * CHUNKS])

    def join_copy(d):
        return pltpu.make_async_remote_copy(
            src_ref=joined.at[sec],
            dst_ref=joined.at[sec],
            send_sem=join_send.at[d],
            recv_sem=join_recv.at[sections - d],
            device_id={"section": (sec + d) % sections},
            device_id_type=MESH,
        )

    def join_arrival(d):
        return pltpu.make_async_remote_copy(
            src_ref=joined.at[sec],
            dst_ref=joined.at[(sec + d) % sections],
            send_sem=join_send.at[d],
            recv_sem=join_recv.at[d],
            device_id={"section": (sec + d) % sections},
            device_id_type=MESH,
        )

    def grad_copy(c):
        wide = gains.shape[0] // KVH * HD
        return pltpu.make_async_copy(
            moved.at[c], grad.at[:, c * wide:(c + 1) * wide], grad_sem.at[c]
        )

    own_h = [
        pltpu.make_async_copy(hid_slice(fx, zz, side), hid.at[side, 0], local_sem.at[side])
        for side in range(2)
    ]

    barrier = pltpu.get_barrier_semaphore()
    everyone = f * n
    me = fx * n + sq

    def greet(d, carry):
        other = (me + d) % everyone
        pl.semaphore_signal(
            barrier, inc=1, device_id={"fsdp": other // n, "seq": other % n}, device_id_type=MESH
        )
        return carry

    lax.fori_loop(1, everyone, greet, 0)
    for d in range(1, sections):
        pl.semaphore_signal(
            barrier, inc=1, device_id={"section": (sec + d) % sections}, device_id_type=MESH
        )
    pl.semaphore_wait(barrier, everyone - 1 + sections - 1)

    def send_hidden(d, carry):
        hid_copy(d, 0).start()
        hid_copy(d, 1).start()
        return carry

    lax.fori_loop(1, group, send_hidden, 0)
    for c in range(CHUNKS):
        w_copy(c, 0).start()
        w_copy(c, 1).start()
    for copy in own_h + own_w + [own_q]:
        copy.start()

    window = (wb + 1) * rows
    i = lax.broadcasted_iota(jnp.int32, (BLK, window), 0)
    j = lax.broadcasted_iota(jnp.int32, (BLK, window), 1) - wb * rows
    for a in range(rows // BLK):
        seen = q_doc[a * BLK:(a + 1) * BLK, :] == k_doc[...]
        seen = seen & (j <= i + a * BLK)
        seen = seen & ((opened[a:a + 1, :] == 1) | (j >= a * BLK))
        bias[a * BLK:(a + 1) * BLK, :] = jnp.where(seen, 0.0, HIDE)

    for j in range(1, wb + 1):
        @pl.when(sq < j)
        def _():
            kvw[wb - j] = jnp.zeros_like(kvw[wb - j])

    for copy in own_h + own_w + [own_q]:
        copy.wait()

    def take_hidden(d, carry):
        hid_arrival(d, 0).wait_recv()
        hid_arrival(d, 1).wait_recv()
        return carry

    lax.fori_loop(1, group, take_hidden, 0)

    def product(c, d):
        return jnp.dot(hid[0, d], wts[0, c], preferred_element_type=jnp.float32) + jnp.dot(
            hid[1, d], wts[1, c], preferred_element_type=jnp.float32
        )

    def middle(c):
        def add(e, carry):
            rs_arrival(c, e).wait_recv()
            own[c, e % hs] += rs[c, e - hs].astype(jnp.float32)
            return carry

        lax.fori_loop(hs, group, add, 0)
        for dz in range(1, hs):
            part2[c, dz] = own[c, dz].astype(jnp.bfloat16)
            along_move(c, dz, hs - dz).start()

    def finish(c):
        for dz in range(1, hs):
            along_move(c, dz, dz).wait_recv()
            own[c, 0] += rs2[c, dz].astype(jnp.float32)
        kvw[wb, c] = own[c, 0].astype(jnp.bfloat16)
        for j in range(1, wb + 1):
            @pl.when(sq + j < n)
            def _():
                ag_copy(c, j).start()

    scale = 1.0 / math.sqrt(HD)
    heads = gains.shape[0] // KVH

    def attend(c, total):
        for j in range(1, wb + 1):
            @pl.when(sq >= j)
            def _():
                ag_copy(c, j).wait_recv()

        k = kvw[:, c, :, :HD].reshape(window, HD)
        v = kvw[:, c, :, HD:].reshape(window, HD)
        gain[...] = lax.dot_general(
            gains[c * heads:(c + 1) * heads, :], v.astype(jnp.float32), (((1,), (1,)), ((), ())),
            precision=lax.Precision.HIGHEST, preferred_element_type=jnp.float32,
        )

        def head(h, total):
            start = pl.multiple_of((c * heads + h) * HD, HD)
            logits = lax.dot_general(
                q[:, pl.ds(start, HD)], k, (((1,), (1,)), ((), ())),
                preferred_element_type=jnp.float32,
            )
            p = jnp.exp2(logits * (scale * math.log2(math.e)) + bias[...])
            u = gain[pl.ds(h, 1), :]
            inverse = 1.0 / jnp.sum(p, axis=1, keepdims=True)
            rho = jnp.sum(p * u, axis=1, keepdims=True) * inverse
            pulled = (p * (u - rho)).astype(jnp.bfloat16)
            pull = jnp.dot(pulled, k, preferred_element_type=jnp.float32) * (scale * inverse)
            moved[c, :, pl.ds(pl.multiple_of(h * HD, HD), HD)] = pull.astype(jnp.bfloat16)
            return total + rho

        def pair(t, total):
            return head(2 * t + 1, head(2 * t, total))

        total = lax.fori_loop(0, heads // 2, pair, total)
        grad_copy(c).start()
        return total

    total = jnp.zeros((rows, 1), jnp.float32)
    for c in range(CHUNKS):
        w_copy(c, 0).wait_recv()
        w_copy(c, 1).wait_recv()

        def place(e):
            g = (fx + e // hs) % f * hs + (zz + e % hs) % hs
            return (g - gi + group) % group

        def spread(e, carry):
            part[c, e - hs] = product(c, place(e)).astype(jnp.bfloat16)
            rs_copy(c, e).start()
            return carry

        lax.fori_loop(hs, group, spread, 0)

        def keep(e, carry):
            own[c, e] = product(c, place(e))
            return carry

        lax.fori_loop(0, hs, keep, 0)
        if c > 0:
            finish(c - 1)
        middle(c)
        if c > 1:
            total = attend(c - 2, total)
    finish(CHUNKS - 1)
    total = attend(CHUNKS - 2, total)
    total = attend(CHUNKS - 1, total)

    row = jnp.transpose(jnp.broadcast_to(total, (rows, HD)))[:8, :]
    joined[sec] = row
    scores[...] = row[:1, :]
    for d in range(1, sections):
        join_copy(d).start()

    def sent(d, carry):
        hid_copy(d, 0).wait_send()
        hid_copy(d, 1).wait_send()
        return carry

    lax.fori_loop(1, group, sent, 0)

    def summed(e, carry):
        for c in range(CHUNKS):
            rs_copy(c, e).wait_send()
        return carry

    lax.fori_loop(hs, group, summed, 0)
    for c in range(CHUNKS):
        w_copy(c, 0).wait_send()
        w_copy(c, 1).wait_send()
        grad_copy(c).wait()
        for dz in range(1, hs):
            along_move(c, dz, hs - dz).wait_send()
        for j in range(1, wb + 1):
            @pl.when(sq + j < n)
            def _():
                ag_copy(c, j).wait_send()
    for d in range(1, sections):
        join_copy(d).wait_send()
        join_arrival(d).wait_recv()
    by_model = [joined[m, :1, :] for m in range(4)]
    actor_part = (sec == 0).astype(jnp.float32)
    critic_part = (sec == 3).astype(jnp.float32)
    actor_term = penalty_weight * (by_model[0] - by_model[1]) - (by_model[2] - by_model[3])
    critic_term = by_model[3] - by_model[2]
    factor[...] = live[...].astype(jnp.float32) * (
        actor_part * actor_term + critic_part * critic_term
    )


def run_step(hidden, weight, queries, gains, q_doc, k_doc, opened, live, f, n, wb, sections):
    rows = hidden.shape[0]
    slab, width = weight.shape
    hs = n // 2
    group = f * hs
    cols = width // CHUNKS
    window = (wb + 1) * rows
    wide = queries.shape[1] // KVH
    dma = pltpu.SemaphoreType.DMA
    hbm = pl.BlockSpec(memory_space=pl.ANY)
    vmem = pl.BlockSpec(memory_space=pltpu.VMEM)
    return pl.pallas_call(
        functools.partial(step_kernel, f, n, wb, sections),
        out_shape=(
            jax.ShapeDtypeStruct(queries.shape, jnp.bfloat16),
            jax.ShapeDtypeStruct((1, rows), jnp.float32),
            jax.ShapeDtypeStruct((1, rows), jnp.float32),
        ),
        in_specs=[hbm] * 3 + [vmem] * 5,
        out_specs=(hbm, vmem, vmem),
        scratch_shapes=[
            pltpu.VMEM((2, group, rows, slab), jnp.bfloat16),
            pltpu.VMEM((2, CHUNKS, slab, cols), jnp.bfloat16),
            pltpu.VMEM((CHUNKS, group - hs, rows, cols), jnp.bfloat16),
            pltpu.VMEM((CHUNKS, group - hs, rows, cols), jnp.bfloat16),
            pltpu.VMEM((CHUNKS, hs, rows, cols), jnp.bfloat16),
            pltpu.VMEM((CHUNKS, hs, rows, cols), jnp.bfloat16),
            pltpu.VMEM((CHUNKS, hs, rows, cols), jnp.float32),
            pltpu.VMEM((wb + 1, CHUNKS, rows, cols), jnp.bfloat16),
            pltpu.VMEM(queries.shape, jnp.bfloat16),
            pltpu.VMEM((KVH, rows, wide), jnp.bfloat16),
            pltpu.VMEM((rows, window), jnp.float32),
            pltpu.VMEM((QH // KVH, window), jnp.float32),
            pltpu.VMEM((sections, 8, rows), jnp.float32),
            dma((2, group)), dma((2, group)),
            dma((CHUNKS, 2)), dma((CHUNKS, 2)),
            dma((CHUNKS, group - hs)), dma((CHUNKS, group - hs)),
            dma((CHUNKS, hs)), dma((CHUNKS, hs)),
            dma((CHUNKS, wb)), dma((CHUNKS, wb)),
            dma((sections,)), dma((sections,)),
            dma((3 + 2 * CHUNKS,)), dma((KVH,)),
        ],
        compiler_params=pltpu.CompilerParams(
            collective_id=0, has_side_effects=True, vmem_limit_bytes=58 * 1024 * 1024
        ),
        cost_estimate=pl.CostEstimate(
            flops=4 * group * rows * slab * width + 4 * rows * queries.shape[1] * window,
            bytes_accessed=2 * hidden.size + 4 * weight.size + 4 * queries.size,
            transcendentals=rows * window * QH,
        ),
    )(hidden, weight, queries, gains, q_doc, k_doc, opened, live)


def on_device(hidden, queries, kv_weight, readout, segments, block_mask, response):
    rows = hidden.shape[1]
    f = lax.axis_size("fsdp")
    n = lax.axis_size("seq")
    sections = lax.axis_size("section")
    seq_len = segments.shape[1]
    wb = -(-(seq_len // 2 - 1) // rows)
    sq = lax.axis_index("seq")
    docs = jnp.concatenate([jnp.full((1, wb * rows), -1, jnp.int32), segments], axis=1)
    k_doc = lax.dynamic_slice_in_dim(docs, sq * rows, (wb + 1) * rows, 1)
    q_doc = k_doc[:, wb * rows:].reshape(rows, 1)
    table = jnp.repeat(jnp.pad(block_mask[0], ((0, 0), (wb * rows // BLK, 0))), BLK, axis=1)
    opened = lax.dynamic_slice_in_dim(table, sq * rows, (wb + 1) * rows, 1)
    grad, token_scores, factor = run_step(
        hidden[0], kv_weight[0], queries[0], readout[0].reshape(QH, HD),
        q_doc, k_doc, opened, response.reshape(1, rows), f, n, wb, sections,
    )
    query_grad = (factor.reshape(rows, 1) * grad.astype(jnp.float32)).astype(jnp.bfloat16)
    return (token_scores, query_grad[None])


def solution(mesh):
    placed = (
        P("section", ("fsdp", "seq"), None),
        P("section", ("fsdp", "seq"), None),
        P("section", ("fsdp", "seq"), None),
        P("section", None),
        P("fsdp", None),
        P("fsdp", "seq", None),
        P(("fsdp", "seq")),
    )
    return jax.shard_map(
        on_device,
        mesh=mesh,
        in_specs=placed,
        out_specs=(P("section", ("fsdp", "seq")), P("section", ("fsdp", "seq"), None)),
        check_vma=False,
    )
```
